32 devices in a mesh: tenant: 2 (over y), blk: 4 (over z), col: 2 (over x), rep: 2 (over core).
Axes of the slice: x: 2, y: 2, z: 4, core: 2. Of those that a mesh axis runs over, the one named last changes fastest.
Arguments:
- picture_projection_source: bfloat16 [3840, 1536], P(('tenant', 'blk', 'rep')), parts along dimension 0, as said below
- caption_projection_source: bfloat16 [3840, 1536], P(('tenant', 'blk')), parts along dimension 0, as said below
- picture_projection_matrix: bfloat16 [1536, 1536], P(None, 'col')
- caption_projection_matrix: bfloat16 [1536, 1536], P(None, 'col')
- picture_projection_offset: float32 [3072], P(('tenant', 'col')), parts along dimension 0, may hold values from -3 to 3
- caption_projection_offset: float32 [3072], P(('tenant', 'col')), parts along dimension 0, may hold values from -3 to 3
- matched_caption_index: int32 [3840], P(('tenant', 'blk', 'rep')), parts along dimension 0, may hold values from 0 to 1919, each once
- sharpness_factor: float32 [2], P('tenant'), parts along dimension 0, may hold values from 10 to 16
- similarity_offset: float32 [2], P('tenant'), parts along dimension 0, may hold values from -8 to -5
- constant_objective_factor: float32 [2], P('tenant'), parts along dimension 0, may hold values from 7680 to 30720
- update_rate_factor: float32 [2], P('tenant'), parts along dimension 0, may hold values from 0.005705443 to 0.022821773
Outputs:
- img_grad: bfloat16 [3840, 1536], P(('tenant', 'blk', 'rep'), 'col'), parts along dimension 0
- txt_grad: bfloat16 [3840, 1536], P(('tenant', 'blk', 'rep'), 'col'), parts along dimension 0
- new_img_bias: float32 [3072], P(('tenant', 'col')), parts along dimension 0
- new_txt_bias: float32 [3072], P(('tenant', 'col')), parts along dimension 0
The draws below stay inside these ranges and needn't reach their ends.
There are 2 independent parts, one for each index of `tenant`. The reference program is written for one: setup_inputs(seed, part) draws one part's arguments, and reference() takes and returns one part's arrays. A program takes and returns all parts, laid end to end along the dimension named above; an argument that names none is the same for every part. Nothing has to cross between parts.
Inputs may be any that keep to these rules, and one draw needn't show every extreme that they name: `matched_caption_index`: every text index is the partner of exactly one image. `picture_projection_source`: row scales differ from row to row. `caption_projection_source`: row scales differ from row to row.
All inputs are finite; a program needn't handle non-finite values.
Results may differ from the reference program's by a relative error of at most 0.0095.
Values may be sent and summed in bfloat16 or wider, within the bound.
No kernel may reach another device: no remote copies, remote signals or barrier semaphores. Data moves between devices by JAX's collectives and lax.ppermute only.
A program may use at most 64 MiB of HBM per device.

```python
import math
import jax
import jax.numpy as jnp
from jax import lax

WIDTH = 1536
EMBED = 1536
TXT_DEV = 480
PAIRS = 1920


def shared_centres(key):
    clusters = max(PAIRS // 16, 4)
    return jax.random.normal(jax.random.fold_in(key, 502), (clusters, WIDTH))


def shared_basis(key):
    return jax.random.normal(jax.random.fold_in(key, 501), (WIDTH, EMBED))


def source_rows(key, centres, low, high, centre_share, noise_share):
    first, second, third = jax.random.split(key, 3)
    member = jax.random.randint(third, (PAIRS,), 0, centres.shape[0])
    scale = jnp.exp(jax.random.uniform(first, (PAIRS, 1), minval=math.log(low), maxval=math.log(high)))
    noise = jax.random.normal(second, (PAIRS, WIDTH))
    values = centre_share * centres[member] + noise_share * noise
    return (scale * values).astype(jnp.bfloat16)


def draw_picture_projection_source(key, part):
    centres = shared_centres(key)
    key = jax.random.fold_in(key, 11)
    return source_rows(key, centres, 0.5, 5.0, 0.9, 0.44)


def draw_caption_projection_source(key, part):
    centres = shared_centres(key)
    key = jax.random.fold_in(key, 12)
    return source_rows(key, centres, 0.5, 5.0, 0.9, 0.44)


def draw_picture_projection_matrix(key, part):
    basis = shared_basis(key)
    key = jax.random.fold_in(key, 21)
    own = jax.random.normal(key, (WIDTH, EMBED))
    return ((0.9 * basis + 0.44 * own) / math.sqrt(WIDTH)).astype(jnp.bfloat16)


def draw_caption_projection_matrix(key, part):
    basis = shared_basis(key)
    key = jax.random.fold_in(key, 22)
    own = jax.random.normal(key, (WIDTH, EMBED))
    return ((0.9 * basis + 0.44 * own) / math.sqrt(WIDTH)).astype(jnp.bfloat16)


def block_levels(rng, extent, shards, low, top_value):
    level, own = 1.0, jax.random.fold_in(rng, 6)
    for axis_at, shards_of in shards:
        steps = jnp.exp(jax.random.uniform(jax.random.fold_in(own, axis_at), (shards_of,), jnp.float32, low / len(shards), top_value / len(shards)))
        level = level * jnp.repeat(steps, extent[axis_at] // shards_of).reshape([-1 if axis == axis_at else 1 for axis in range(len(extent))])
    return level


def bell_draw(stream_key, extent, spread, reach, shards=(), held_as=jnp.bfloat16):
    drawn = jax.random.normal(stream_key, extent, jnp.float32) * spread
    if len(shards) > 0:
        drawn = block_levels(stream_key, extent, shards, -0.22, 0.18) * drawn
    return jnp.clip(drawn, min=-reach, max=reach).astype(held_as)


def setup_inputs(seed: int = 0, part: int = 0) -> dict:
    seeds = jax.random.split(jax.random.key(seed), 12)
    part_splits = jax.random.split(jax.random.fold_in(seeds[11], part), 12)
    return {
        "picture_projection_source": draw_picture_projection_source(jax.random.fold_in(jax.random.fold_in(seeds[11], part), 71), part),
        "caption_projection_source": draw_caption_projection_source(jax.random.fold_in(jax.random.fold_in(seeds[11], part), 71), part),
        "picture_projection_matrix": draw_picture_projection_matrix(jax.random.fold_in(seeds[11], 71), part),
        "caption_projection_matrix": draw_caption_projection_matrix(jax.random.fold_in(seeds[11], 71), part),
        "picture_projection_offset": bell_draw(part_splits[4], (EMBED,), 0.5, 3.0, ((0, 2),), jnp.float32),
        "caption_projection_offset": bell_draw(part_splits[5], (EMBED,), 0.5, 3.0, ((0, 2),), jnp.float32),
        "matched_caption_index": jax.random.permutation(part_splits[6], PAIRS).astype(jnp.int32),
        "sharpness_factor": jnp.clip(jax.random.uniform(part_splits[7], (1,), jnp.float32, 10.0, 16.0), 10.0, 16.0),
        "similarity_offset": jnp.clip(jax.random.uniform(part_splits[8], (1,), jnp.float32, -8.0, -5.0), -8.0, -5.0),
        "constant_objective_factor": jnp.clip(jnp.exp(jax.random.uniform(part_splits[9], (1,), jnp.float32, math.log(7680.0), math.log(30720.0))), 7680.0, 30720.0),
        "update_rate_factor": jnp.clip(jnp.exp(jax.random.uniform(part_splits[10], (1,), jnp.float32, math.log(0.005705443), math.log(0.022821773))), 0.005705443, 0.022821773),
    }


EPS = 1e-06

def tower(inputs, coefficient_matrix, bias):
    pre = jnp.dot(inputs, coefficient_matrix, preferred_element_type=jnp.float32) + bias
    inv = lax.rsqrt(lax.optimization_barrier(jnp.sum(pre * pre, axis=1, keepdims=True)) + EPS)
    return (inv, (pre * inv).astype(jnp.bfloat16))

def reference(picture_projection_source, caption_projection_source, picture_projection_matrix, caption_projection_matrix, picture_projection_offset, caption_projection_offset, matched_caption_index, sharpness_factor, similarity_offset, constant_objective_factor, update_rate_factor):
    img_inv, img_z = tower(picture_projection_source, picture_projection_matrix, picture_projection_offset)
    txt_inv, caption_embedding_vector = tower(caption_projection_source, caption_projection_matrix, caption_projection_offset)
    similarity_sharpness = sharpness_factor[0]
    offset_coefficient = similarity_offset[0]
    coef = constant_objective_factor[0] / PAIRS
    group = TXT_DEV
    count = PAIRS // group
    columns = jnp.arange(PAIRS, dtype=jnp.int32)
    blocks_z = img_z.reshape(count, group, EMBED)
    blocks_p = matched_caption_index.reshape(count, group)

    def step(carry, item):
        running_total, col_acc = carry
        similarity_tile, pblock = item
        pairwise_similarity = similarity_sharpness * jnp.dot(similarity_tile, caption_embedding_vector.T, preferred_element_type=jnp.float32) + offset_coefficient
        label = jnp.where(pblock[:, None] == columns[None, :], 1.0, -1.0).astype(jnp.float32)
        coefficient_matrix = (-coef * label * jax.nn.sigmoid(-label * pairwise_similarity)).astype(jnp.bfloat16)
        weighted = coefficient_matrix.astype(jnp.float32) * (pairwise_similarity - offset_coefficient)
        pairwise_derivative_tile = similarity_sharpness * jnp.dot(coefficient_matrix, caption_embedding_vector, preferred_element_type=jnp.float32)
        running_total = running_total + similarity_sharpness * jnp.dot(coefficient_matrix.T, similarity_tile, preferred_element_type=jnp.float32)
        col_acc = col_acc + lax.optimization_barrier(jnp.sum(weighted, axis=0))
        return ((running_total, col_acc), (pairwise_derivative_tile, lax.optimization_barrier(jnp.sum(weighted, axis=1))))
    init = (jnp.zeros((PAIRS, EMBED), jnp.float32), jnp.zeros((PAIRS,), jnp.float32))
    (txt_dz, col_dot), (img_dz, row_dot) = lax.scan(step, init, (blocks_z, blocks_p))
    img_dz = img_dz.reshape(PAIRS, EMBED)
    row_dot = row_dot.reshape(PAIRS)
    img_dpre = img_inv * (img_dz - img_z.astype(jnp.float32) * row_dot[:, None])
    txt_dpre = txt_inv * (txt_dz - caption_embedding_vector.astype(jnp.float32) * col_dot[:, None])
    img_grad = jnp.dot(img_dpre.astype(jnp.bfloat16), picture_projection_matrix.T, preferred_element_type=jnp.float32).astype(jnp.bfloat16)
    txt_grad = jnp.dot(txt_dpre.astype(jnp.bfloat16), caption_projection_matrix.T, preferred_element_type=jnp.float32).astype(jnp.bfloat16)
    new_img_bias = picture_projection_offset - update_rate_factor[0] * lax.optimization_barrier(jnp.sum(img_dpre, axis=0))
    new_txt_bias = caption_projection_offset - update_rate_factor[0] * lax.optimization_barrier(jnp.sum(txt_dpre, axis=0))
    return (img_grad, txt_grad, new_img_bias, new_txt_bias)
```

```python
import jax
import jax.numpy as jnp
from jax import lax
from jax.sharding import PartitionSpec as P

EPS = 1e-06
F32 = jnp.float32
BF16 = jnp.bfloat16
NT = (((1,), (1,)), ((), ()))
TN = (((0,), (0,)), ((), ()))


def rotated(block, axis, distance):
    count = lax.axis_size(axis)
    return lax.ppermute(block, axis, [(i, (i + distance) % count) for i in range(count)])


def ring_order(count):
    if count <= 4:
        return list(range(0, count, 1)) if count < 4 else [0, 1, 3, 2]
    return list(range(count))


def rows_of(block, start, size):
    return lax.dynamic_slice_in_dim(block, start, size, 0)


def unit_rows(pre):
    wide = pre.astype(F32)
    inv = lax.rsqrt(jnp.sum(wide * wide, axis=1, keepdims=True) + EPS)
    return inv, (wide * inv).astype(BF16)


def tangent(inv, z, dz):
    wide = z.astype(F32)
    return inv * (dz - wide * jnp.sum(wide * dz, axis=1, keepdims=True))


def butterfly(block, axis):
    count, step = lax.axis_size(axis), 1
    while step < count:
        block = block + lax.ppermute(block, axis, [(i, i ^ step) for i in range(count)])
        step *= 2
    return block


def per_device(
    img_source,
    txt_source,
    img_matrix,
    txt_matrix,
    img_offset,
    txt_offset,
    matched,
    sharpness_factor,
    similarity_offset,
    constant_objective_factor,
    update_rate_factor,
):
    rows, group, feats = img_source.shape[0], txt_source.shape[0], img_matrix.shape[1]
    cols, reps, blks = lax.axis_size("col"), lax.axis_size("rep"), lax.axis_size("blk")
    c, r, me = lax.axis_index("col"), lax.axis_index("rep"), lax.axis_index("blk")
    sub = rows // cols
    sharp = sharpness_factor[0]
    offset = similarity_offset[0]
    coef = constant_objective_factor[0] / (rows * blks * reps)

    txt_pre = (
        jnp.dot(rows_of(txt_source, r * rows, rows), txt_matrix, preferred_element_type=F32)
        + txt_offset
    ).astype(BF16)
    txt_parts = [rows_of(txt_pre, c * sub, sub)]
    for d in range(1, cols):
        part = rows_of(txt_pre, ((c + d) % cols) * sub, sub)
        txt_parts.append(rotated(part, "col", d))
    txt_inv, txt_z = unit_rows(jnp.concatenate(txt_parts, axis=1))

    img_pre = (jnp.dot(img_source, img_matrix, preferred_element_type=F32) + img_offset).astype(BF16)
    img_parts = [img_pre] + [rotated(img_pre, "col", d) for d in range(1, cols)]
    img_inv, img_own = unit_rows(jnp.concatenate(img_parts, axis=1))
    img_z = jnp.concatenate([img_own] + [rotated(img_own, "rep", d) for d in range(1, reps)], axis=0)
    labels = jnp.concatenate([matched] + [rotated(matched, "rep", d) for d in range(1, reps)], axis=0)

    order = ring_order(blks)
    place = [order.index(i) for i in range(blks)]
    ring = [(order[i], order[(i + 1) % blks]) for i in range(blks)]
    position = jnp.array(place, jnp.int32)[me]

    def pair_weights(text, source):
        first = source * group + r * rows + c * sub
        column = first + lax.broadcasted_iota(jnp.int32, (1, sub), 1)
        label = jnp.where(labels[:, None] == column, 1.0, -1.0).astype(F32)
        logit = sharp * lax.dot_general(img_z, text, NT, preferred_element_type=F32) + offset
        return (-coef * label * jax.nn.sigmoid(-label * logit)).astype(BF16)

    texts, weights = [txt_z], []
    for _ in range(1, blks):
        texts.append(lax.ppermute(texts[-1], "blk", ring))
    total = None
    for k in list(range(1, blks)) + [0]:
        source = jnp.array(order, jnp.int32)[(position - k) % blks]
        weight = pair_weights(texts[k], source)
        weights.append((k, weight))
        part = sharp * lax.dot_general(weight, img_z, TN, preferred_element_type=F32)
        if total is not None:
            part = part + total.astype(F32)
        if k:
            total = lax.ppermute(part.astype(BF16), "blk", ring)
        else:
            txt_dz = part

    img_dz = sharp * jnp.dot(
        jnp.concatenate([w for _, w in weights], axis=1),
        jnp.concatenate([texts[k] for k, _ in weights], axis=0),
        preferred_element_type=F32,
    )
    own = img_dz[:rows]
    for d in range(1, reps):
        sent = img_dz[d * rows : (d + 1) * rows]
        own = own + rotated(sent.astype(BF16), "rep", reps - d).astype(F32)
    kept = rows_of(own, c * sub, sub)
    for d in range(1, cols):
        part = rows_of(own, ((c + d) % cols) * sub, sub).astype(BF16)
        cut = (cols - d) * feats
        part = jnp.concatenate([part[:, cut:], part[:, :cut]], axis=1)
        kept = kept + rotated(part, "col", d).astype(F32)

    img_dpre = tangent(rows_of(img_inv, c * sub, sub), rows_of(img_own, c * sub, sub), kept)
    txt_dpre = tangent(txt_inv, txt_z, txt_dz)

    def all_rows(dpre):
        dpre = dpre.astype(BF16)
        whole = jnp.zeros((rows, feats), BF16)
        whole = lax.dynamic_update_slice_in_dim(whole, dpre[:, :feats], c * sub, 0)
        for d in range(1, cols):
            part = rotated(dpre[:, d * feats : (d + 1) * feats], "col", cols - d)
            whole = lax.dynamic_update_slice_in_dim(whole, part, ((c + d) % cols) * sub, 0)
        return whole

    def input_grad(dpre, matrix):
        part = lax.dot_general(dpre, matrix, NT, preferred_element_type=F32)
        width = part.shape[1] // cols
        grad = lax.dynamic_slice_in_dim(part, c * width, width, 1)
        for d in range(1, cols):
            sent = lax.dynamic_slice_in_dim(part, ((c + d) % cols) * width, width, 1).astype(BF16)
            grad = grad + rotated(sent, "col", d).astype(F32)
        return grad.astype(BF16)

    img_rows, txt_rows = all_rows(img_dpre), all_rows(txt_dpre)
    img_grad = input_grad(img_rows, img_matrix)
    txt_grad = input_grad(txt_rows, txt_matrix)
    sums = jnp.stack([jnp.sum(img_rows.astype(F32), axis=0), jnp.sum(txt_rows.astype(F32), axis=0)])
    sums = butterfly(butterfly(sums, "rep"), "blk")
    rate = update_rate_factor[0]
    return (img_grad, txt_grad, img_offset - rate * sums[0], txt_offset - rate * sums[1])


def solution(mesh):
    in_specs = (
        P(("tenant", "blk", "rep"), None),
        P(("tenant", "blk"), None),
        P(None, "col"),
        P(None, "col"),
        P(("tenant", "col")),
        P(("tenant", "col")),
        P(("tenant", "blk", "rep")),
        P("tenant"),
        P("tenant"),
        P("tenant"),
        P("tenant"),
    )
    out_specs = (
        P(("tenant", "blk", "rep"), "col"),
        P(("tenant", "blk", "rep"), "col"),
        P(("tenant", "col")),
        P(("tenant", "col")),
    )
    return jax.shard_map(
        per_device, mesh=mesh, in_specs=in_specs, out_specs=out_specs, check_vma=False
    )
```

```python
import jax
import jax.numpy as jnp
from jax import lax
from jax.sharding import PartitionSpec as P

EPS = 1e-06
F32 = jnp.float32
BF16 = jnp.bfloat16
NT = (((1,), (1,)), ((), ()))
TN = (((0,), (0,)), ((), ()))


def rotated(block, axis, distance):
    count = lax.axis_size(axis)
    return lax.ppermute(block, axis, [(i, (i + distance) % count) for i in range(count)])


def rows_of(block, start, size):
    return lax.dynamic_slice_in_dim(block, start, size, 0)


def unit_rows(pre):
    wide = pre.astype(F32)
    inv = lax.rsqrt(jnp.sum(wide * wide, axis=1, keepdims=True) + EPS)
    return inv, (wide * inv).astype(BF16)


def tangent(inv, z, dz):
    wide = z.astype(F32)
    return inv * (dz - wide * jnp.sum(wide * dz, axis=1, keepdims=True))


def after(value, *others):
    return lax.optimization_barrier((value, *others))[0]


def all_summed(block, axis):
    step = 1
    while step < lax.axis_size(axis):
        block = block + across(block, axis, step)
        step *= 2
    return block


def across(block, axis, step):
    return lax.ppermute(block, axis, [(i, i ^ step) for i in range(lax.axis_size(axis))])


def share_of(matrix):
    tenants, reps = lax.axis_size("tenant"), lax.axis_size("rep")
    place = lax.axis_index("tenant") * reps + lax.axis_index("rep")
    size = matrix.shape[0] // (tenants * reps)
    return rows_of(matrix, place * size, size)


def over_tenants(share):
    return [share] + [rotated(share, "tenant", e) for e in range(1, lax.axis_size("tenant"))]


def over_reps(shares):
    tenants, reps = lax.axis_size("tenant"), lax.axis_size("rep")
    y, r = lax.axis_index("tenant"), lax.axis_index("rep")
    size, width = shares[0].shape
    whole = jnp.zeros((tenants * reps * size, width), shares[0].dtype)
    shares = jnp.concatenate(shares, axis=0)
    for f in range(reps):
        got = rotated(shares, "rep", f) if f else shares
        for e in range(tenants):
            place = ((y + tenants - e) % tenants) * reps + (r + reps - f) % reps
            whole = lax.dynamic_update_slice_in_dim(whole, got[e * size : (e + 1) * size], place * size, 0)
    return whole


def per_device(
    img_source,
    txt_source,
    img_matrix,
    txt_matrix,
    img_offset,
    txt_offset,
    matched,
    sharpness_factor,
    similarity_offset,
    constant_objective_factor,
    update_rate_factor,
):
    rows, group, feats = img_source.shape[0], txt_source.shape[0], img_matrix.shape[1]
    cols, reps, blks = lax.axis_size("col"), lax.axis_size("rep"), lax.axis_size("blk")
    c, r, me = lax.axis_index("col"), lax.axis_index("rep"), lax.axis_index("blk")
    sub = rows // cols
    sharp = sharpness_factor[0]
    offset = similarity_offset[0]
    coef = constant_objective_factor[0] / (rows * blks * reps)

    txt_pre = (
        jnp.dot(rows_of(txt_source, r * rows, rows), txt_matrix, preferred_element_type=F32)
        + txt_offset
    ).astype(BF16)
    txt_parts = [rows_of(txt_pre, c * sub, sub)]
    for d in range(1, cols):
        part = rows_of(txt_pre, ((c + d) % cols) * sub, sub)
        txt_parts.append(rotated(part, "col", d))
    texts = [jnp.concatenate(txt_parts, axis=1)]

    img_pre = (
        jnp.dot(after(img_source, txt_pre), img_matrix, preferred_element_type=F32) + img_offset
    ).astype(BF16)
    labels = jnp.concatenate([matched] + [rotated(matched, "rep", d) for d in range(1, reps)], axis=0)

    def all_columns(block):
        return jnp.concatenate([block] + [rotated(block, "col", d) for d in range(1, cols)], axis=1)

    def all_images(own):
        every = jnp.concatenate([own] + [rotated(own, "rep", d) for d in range(1, reps)], axis=0)
        return lax.optimization_barrier(unit_rows(every))

    route = [0, 1, 3, 2] if blks == 4 else list(range(blks))
    route = [(route[i], route[(i + 1) % blks]) for i in range(blks)]

    def pair_weights(text, source):
        first = source * group + r * rows + c * sub
        column = first + lax.broadcasted_iota(jnp.int32, (1, sub), 1)
        label = jnp.where(labels[:, None] == column, 1.0, -1.0).astype(F32)
        logit = sharp * lax.dot_general(img_z, text, NT, preferred_element_type=F32) + offset
        return (-coef * label * jax.nn.sigmoid(-label * logit)).astype(BF16)

    units, weights, parts = {}, {}, {}

    def source_of(distance):
        if blks == 4:
            place = ((me ^ (me >> 1)) + blks - distance) % blks
            return place ^ (place >> 1)
        return (me + blks - distance) % blks

    def work(k, text, distance):
        source = source_of(distance)
        inv, units[k] = unit_rows(text)
        weights[k] = pair_weights(units[k], source)
        part = sharp * lax.dot_general(weights[k], img_z, TN, preferred_element_type=F32)
        parts[k] = lax.optimization_barrier(tangent(inv, units[k], lax.optimization_barrier(part)))

    def image_part():
        img_dz = sharp * jnp.dot(
            jnp.concatenate([weights[k] for k in range(blks)], axis=1),
            jnp.concatenate([units[k] for k in range(blks)], axis=0),
            preferred_element_type=F32,
        )
        dpre = tangent(img_inv, img_z, img_dz)
        return dpre, jnp.stack([jnp.sum(dpre, axis=0), jnp.sum(sum(parts.values()), axis=0)])

    def from_reps(block):
        return [
            rotated(block[d * rows : (d + 1) * rows].astype(BF16), "rep", reps - d)
            for d in range(1, reps)
        ]

    def from_columns(block):
        return [rotated(block[:, d * feats : (d + 1) * feats], "col", cols - d) for d in range(1, cols)]

    def added(block, others):
        for other in others:
            block = block + other.astype(F32)
        return block

    def ring(block):
        return lax.ppermute(block, "blk", route)

    together = lax.optimization_barrier
    last = blks - 1
    cut = max(sub // 2 // 16, 1) * 16
    upper, lower = [texts[0][:cut]], [texts[0][cut:]]

    def moved(k):
        return jnp.concatenate([upper[k], lower[k]], axis=0)

    for k in range(1, blks):
        upper.append(ring(upper[-1]))
        lower.append(ring(lower[-1]))
        if k == 1:
            lower[1], img_own = together((lower[1], all_columns(img_pre)))
            shares = [rotated(after(share_of(txt_matrix), img_own), "col", d) for d in range(1, cols)]
            img_inv, img_z = all_images(img_own)
        else:
            work(k - 2, moved(k - 2), k - 2)
            if k == last:
                work(k - 1, moved(k - 1), k - 1)
                keep = [parts[j] for j in range(k)]
                upper[k], lower[k], shares, keep = together((upper[k], lower[k], shares, keep))
                parts.update(enumerate(keep))
            else:
                lower[k], parts[k - 2] = together((lower[k], parts[k - 2]))

    def passed(block, k):
        upper, lower = parts[k][:cut], parts[k][cut:]
        return [
            (part + ring(piece).astype(F32)).astype(BF16) for part, piece in zip((upper, lower), block)
        ]

    line = blks == 4
    steps = [k for k in range(2, blks)] + [0]
    total = [parts[min(last, 1)][:cut].astype(BF16), parts[min(last, 1)][cut:].astype(BF16)]
    total = passed(total, steps[0]) if last else total
    work(last, moved(last), last)
    img_part, sums = image_part()
    img_got, sums_got = from_reps(img_part), [across(sums, "rep", 1)] if reps == 2 else []
    total[1], img_part, img_got, sums, sums_got, parts = together(
        (total[1], img_part, img_got, sums, sums_got, parts)
    )
    own, sums = added(img_part[:rows], img_got), added(sums, sums_got)
    if len(steps) > 1:
        total = passed(total, steps[1])
    img_got = from_columns(own.astype(BF16))
    sums_got = [across(sums, "blk", 1)] if line else []
    shares = [over_tenants(share) for share in shares]
    total[1], img_got, sums, sums_got, shares, parts = together(
        (total[1], img_got, sums, sums_got, shares, parts)
    )
    sums = added(sums, sums_got) if line else all_summed(sums, "blk")
    img_dpre = added(own[:, :feats], img_got).astype(BF16)
    for k in steps[2:]:
        total = passed(total, k)
    width = img_matrix.shape[0] // cols
    part = lax.dot_general(img_dpre, img_matrix, NT, preferred_element_type=F32)
    img_grad = lax.dynamic_slice_in_dim(part, c * width, width, 1)
    img_got = [
        rotated(
            lax.dynamic_slice_in_dim(part, ((c + d) % cols) * width, width, 1).astype(BF16), "col", d
        )
        for d in range(1, cols)
    ]
    sums_got = from_columns(sums)
    whole = jnp.concatenate([txt_matrix] + [over_reps(share) for share in shares], axis=1)
    whole = [rows_of(whole, ((c + d) % cols) * width, width) for d in range(cols)]
    total, img_got, sums, sums_got, whole = together((total, img_got, sums, sums_got, whole))
    txt_dpre = jnp.concatenate(total, axis=0)
    img_grad, sums = added(img_grad, img_got), added(sums[:, :feats], sums_got)
    if line:
        sums = sums + across(sums, "blk", 2)

    part = [
        lax.dot_general(txt_dpre, whole[d], NT, preferred_element_type=F32).astype(BF16)
        for d in range(cols)
    ]
    part = [part[0]] + [rotated(part[d], "col", d) for d in range(1, cols)]
    txt_grad = jnp.zeros((rows, width), BF16)
    for d in range(cols):
        at = ((c + cols - d) % cols) * sub
        txt_grad = lax.dynamic_update_slice_in_dim(txt_grad, part[d], at, 0)

    rate = update_rate_factor[0]
    return (
        img_grad.astype(BF16),
        txt_grad,
        img_offset - rate * sums[0],
        txt_offset - rate * sums[1],
    )


def solution(mesh):
    in_specs = (
        P(("tenant", "blk", "rep"), None),
        P(("tenant", "blk"), None),
        P(None, "col"),
        P(None, "col"),
        P(("tenant", "col")),
        P(("tenant", "col")),
        P(("tenant", "blk", "rep")),
        P("tenant"),
        P("tenant"),
        P("tenant"),
        P("tenant"),
    )
    out_specs = (
        P(("tenant", "blk", "rep"), "col"),
        P(("tenant", "blk", "rep"), "col"),
        P(("tenant", "col")),
        P(("tenant", "col")),
    )
    return jax.shard_map(
        per_device, mesh=mesh, in_specs=in_specs, out_specs=out_specs, check_vma=False
    )
```
